128 devices in a mesh: tile: 64 (over y, z, x), gene: 2 (over core).
Axes of the slice: x: 4, y: 4, z: 4, core: 2. Of those that a mesh axis runs over, the one named last changes fastest.
Arguments:
- source_expr: bfloat16 [2000, 196608], P('gene', 'tile'), may hold values from -6 to 6
- target_expr: bfloat16 [2000, 196608], P('gene', 'tile'), may hold values from -6 to 6
- prior_plan: bfloat16 [1536, 8, 128, 128], P('tile'), may hold values from 0.01 to 46
- nonzero_pattern: int32 [1536, 8], P('tile'), may hold values from 0 to 1535, as said below
- live: int32 [1536], P('tile'), may hold values from 1 to 8, as said below
- source_mass: float32 [196608], P('tile'), may hold values from 0.2 to 5
- target_mass: float32 [196608], P('tile'), may hold values from 0.2 to 5
- initial_logarithm_right: float32 [196608], P('tile'), may hold values from -4 to 263
Outputs:
- logarithm_left_factors: float32 [196608], P('tile')
- logarithm_right_factors: float32 [196608], P('tile')
The draws below stay inside these ranges and needn't reach their ends.
Inputs may be any that keep to these rules, and one draw needn't show every extreme that they name: nonzero_pattern[n, 0] is n; the other entries of row n are distinct bins, none equal to n, of the tile of bin n or of an adjacent tile (bin n lies in tile n div 24). Some source bin has all 8 blocks live.
All inputs are finite; a program needn't handle non-finite values.
Results may differ from the reference program's by a relative error of at most 0.0003.
Values may be sent and summed in bfloat16 or wider, within the bound.
No kernel may reach another device: no remote copies, remote signals or barrier semaphores. Data moves between devices by JAX's collectives and lax.ppermute only.
A program may use at most 192 MiB of HBM per device.

```python
import math
import jax
import jax.numpy as jnp
from jax import lax

G = 2000
UNITS_IN_GROUP = 128
BINS_DEV = 24
SLOTS = 8
ITERS = 3
SLICE_GROUPS = 1536
NCELLS = 196608


def draw_prior_plan(key, part):
    first, second = jax.random.split(key)
    scale = jnp.exp(jax.random.uniform(first, (SLICE_GROUPS, 1, 1, 1), jnp.float32, -2.3, 2.3))
    entry = jnp.exp(jax.random.uniform(second, (SLICE_GROUPS, SLOTS, UNITS_IN_GROUP, UNITS_IN_GROUP), jnp.float32, -0.7, 0.7))
    return (scale * entry).astype(jnp.bfloat16)


def draw_nonzero_pattern(key, part):
    span = 3 * BINS_DEV
    bins = jnp.arange(SLICE_GROUPS, dtype=jnp.int32)
    tiles = bins // BINS_DEV
    offset = jnp.arange(span, dtype=jnp.int32)
    cand = (tiles[:, None] - 1) * BINS_DEV + offset[None, :]
    invalid = (cand < 0) | (cand >= SLICE_GROUPS) | (cand == bins[:, None])
    scores = jax.random.randint(key, (SLICE_GROUPS, span), 0, 2 ** 20) * span + offset[None, :]
    ranked = scores + invalid.astype(jnp.int32) * 2 ** 29
    order = jnp.argsort(ranked, axis=1)
    picked = jnp.take_along_axis(cand, order[:, :SLOTS - 1], axis=1)
    return jnp.concatenate([bins[:, None], picked], axis=1).astype(jnp.int32)


def draw_live(key, part):
    first, second, third = jax.random.split(key, 3)
    tiles = SLICE_GROUPS // BINS_DEV
    depth = jax.random.randint(first, (tiles,), SLOTS // 2, SLOTS + 1)
    bins = jnp.arange(SLICE_GROUPS, dtype=jnp.int32)
    count = 1 + jax.random.randint(second, (SLICE_GROUPS,), 0, 2 ** 20) % depth[bins // BINS_DEV]
    chosen = jax.random.randint(third, (), 0, SLICE_GROUPS)
    return jnp.where(bins == chosen, SLOTS, count).astype(jnp.int32)


def draw_initial_logarithm_right(key, part):
    first = jax.random.fold_in(key, 0)
    return jnp.clip(jax.random.normal(first, (SLICE_GROUPS * UNITS_IN_GROUP,), jnp.float32), -4.0, 4.0)


def shard_levels(key, extent, cuts, smallest, top_value):
    def one(position, blocks):
        heights = jax.random.uniform(jax.random.fold_in(jax.random.fold_in(key, 6), position), (blocks,), jnp.float32, smallest / len(cuts), top_value / len(cuts))
        return jnp.repeat(jnp.exp(heights), extent[position] // blocks).reshape((-1,) + (1,) * (len(extent) - position - 1))

    factor_of = one(*cuts[0])
    for cut in cuts[1:]:
        factor_of = factor_of * one(*cut)
    return factor_of


def gaussian(stream_key, dims, spread, reach, cuts=(), held_as=jnp.bfloat16):
    drawn = spread * jax.random.normal(stream_key, dims, jnp.float32)
    if cuts:
        drawn = drawn * shard_levels(stream_key, dims, cuts, -0.22, 0.18)
    return jnp.clip(drawn, -reach, reach).astype(held_as)


def setup_inputs(seed: int = 0) -> dict:
    key_of = jax.random.split(jax.random.key(seed), 9)
    return {
        "source_expr": gaussian(key_of[0], (G, NCELLS), 1.0, 6.0, ((0, 2), (1, 64))),
        "target_expr": gaussian(key_of[1], (G, NCELLS), 1.0, 6.0, ((0, 2), (1, 64))),
        "prior_plan": draw_prior_plan(jax.random.fold_in(key_of[8], 71), 0),
        "nonzero_pattern": draw_nonzero_pattern(jax.random.fold_in(key_of[8], 71), 0),
        "live": draw_live(jax.random.fold_in(key_of[8], 71), 0),
        "source_mass": jnp.clip(jnp.exp(math.log(5.0) - 3.218876 * jax.random.uniform(key_of[5], (NCELLS,), jnp.float32) ** shard_levels(key_of[5], (NCELLS,), ((0, 64),), -0.2, 0.2)), 0.2, 5.0),
        "target_mass": jnp.clip(jnp.exp(math.log(5.0) - 3.218876 * jax.random.uniform(key_of[6], (NCELLS,), jnp.float32) ** shard_levels(key_of[6], (NCELLS,), ((0, 64),), -0.2, 0.2)), 0.2, 5.0),
        "initial_logarithm_right": draw_initial_logarithm_right(jax.random.fold_in(key_of[8], 71), 0),
    }


EPS = 0.02
THETA = 0.1
MINUS_HUGE = -1e30


def place_rows(bins, nbins):
    cell = jnp.arange(UNITS_IN_GROUP, dtype=jnp.int32)
    along = ((cell % 16).astype(jnp.float32) + 0.5) / 16.0
    xpos = (bins[..., None].astype(jnp.float32) + along) / nbins
    ypos = jnp.broadcast_to(((cell // 16).astype(jnp.float32) + 0.5) / (16.0 * nbins), xpos.shape)
    radius = xpos * xpos + ypos * ypos
    ones = jnp.ones_like(xpos)
    moment_rows = jnp.stack([ones, radius, xpos, ypos], axis=-1)
    dist_rows = jnp.stack([radius, ones, -2.0 * xpos, -2.0 * ypos], axis=-1)
    return moment_rows, dist_rows


def reference(source_expr, target_expr, prior_plan, nonzero_pattern, live, source_mass, target_mass, initial_logarithm_right):
    hi = lax.Precision.HIGHEST
    bins = jnp.arange(SLICE_GROUPS, dtype=jnp.int32)
    u_mom, u_dist = place_rows(bins, SLICE_GROUPS)
    v_mom = u_mom[nonzero_pattern]
    v_dist = u_dist[nonzero_pattern]
    alive_indicator = jnp.arange(SLOTS, dtype=jnp.int32)[None, :] < live[:, None]
    live_weight = alive_indicator.astype(jnp.float32)

    def block_moments(args):
        plan, urow, vrow, weight = args
        plan_f = plan.astype(jnp.float32) * weight[:, None, None]
        pv = jnp.einsum('kij,kjd->kid', plan_f, vrow, precision=hi)
        return jnp.einsum('ic,kid->cd', urow, pv, precision=hi)

    moments = jnp.sum(lax.map(block_moments, (prior_plan, u_mom, v_mom, live_weight)), axis=0)
    scaled = moments / moments[0, 0]
    target_bins = target_expr.reshape(G, SLICE_GROUPS, UNITS_IN_GROUP)

    def block_cost(args):
        index, targets, udist, vdist = args
        block = lax.dynamic_slice_in_dim(source_expr, (index * UNITS_IN_GROUP).astype(jnp.int32), UNITS_IN_GROUP, 1).astype(jnp.float32)
        chosen = jnp.take(target_bins, targets, axis=1).astype(jnp.float32)
        inner = jnp.einsum('gi,gkj->kij', block, chosen)
        left = jnp.dot(udist, scaled, precision=hi)
        gw = jnp.einsum('id,kjd->kij', left, vdist, precision=hi)
        return -inner / G + THETA * gw

    coupling_price = lax.map(block_cost, (bins, nonzero_pattern, u_dist, v_dist))
    logarithm_left_masses = jnp.log(source_mass).reshape(SLICE_GROUPS, UNITS_IN_GROUP)
    logarithm_marginal_right = jnp.log(target_mass)
    logarithm_right_factors = initial_logarithm_right
    logarithm_left_factors = jnp.zeros((SLICE_GROUPS, UNITS_IN_GROUP), jnp.float32)
    flat_targets = nonzero_pattern.reshape(-1)
    for step in range(ITERS):
        picked_right_factors = logarithm_right_factors.reshape(SLICE_GROUPS, UNITS_IN_GROUP)[nonzero_pattern]

        def left_line_panel(args):
            cb, vb, lm = args
            rating_value = jnp.where(lm[:, None, None], vb[:, None, :] - cb / EPS, MINUS_HUGE)
            top = jnp.max(rating_value, axis=(0, 2))
            return top + jnp.log(jnp.sum(jnp.exp(rating_value - top[None, :, None]), axis=(0, 2)))

        logarithm_left_factors = logarithm_left_masses - lax.map(left_line_panel, (coupling_price, picked_right_factors, alive_indicator))

        def column_panel(args):
            cb, ub, lm = args
            rating_value = jnp.where(lm[:, None, None], ub[None, :, None] - cb / EPS, MINUS_HUGE)
            top = jnp.max(rating_value, axis=1)
            grand_aggregate = jnp.sum(jnp.exp(rating_value - top[:, None, :]), axis=1)
            return top, jnp.where(lm[:, None], grand_aggregate, 0.0)

        maxima_list, aggregate_list = lax.map(column_panel, (coupling_price, logarithm_left_factors, alive_indicator))
        maxima_list = maxima_list.reshape(SLICE_GROUPS * SLOTS, UNITS_IN_GROUP)
        aggregate_list = aggregate_list.reshape(SLICE_GROUPS * SLOTS, UNITS_IN_GROUP)
        largest_found = jax.ops.segment_max(maxima_list, flat_targets, num_segments=SLICE_GROUPS)
        accumulated = jax.ops.segment_sum(aggregate_list * jnp.exp(maxima_list - largest_found[flat_targets]), flat_targets, num_segments=SLICE_GROUPS)
        logarithm_right_factors = logarithm_marginal_right - (largest_found + jnp.log(accumulated)).reshape(-1)
    return logarithm_left_factors.reshape(-1), logarithm_right_factors
```

```python
import functools
import math

import jax
import jax.numpy as jnp
import numpy as np
from jax import lax
from jax.experimental import pallas as pl
from jax.experimental.pallas import tpu as pltpu
from jax.sharding import PartitionSpec as P

G = 2000
ITERS = 3
EPS = 0.02
THETA = 0.1
MINUS_HUGE = -1e30
FEATURES = 6
HI = lax.Precision.HIGHEST
FULL_VMEM = 60 * 2**20
SCALE_VMEM = 12 * 2**20
SMALL_COST = pl.CostEstimate(flops=2**20, bytes_accessed=2**16, transcendentals=0)
TOGETHER = 4
CHUNKS = (4, 9, 8, 3)
PEAK_MAX = 30.0
SCALING_MAX = 40.0
LOG_SUM_MAX = 50.0


def place_rows(bins, nbins, cells):
    cell = jnp.arange(cells, dtype=jnp.int32)
    along = ((cell % 16).astype(jnp.float32) + 0.5) / 16.0
    xpos = (bins[..., None].astype(jnp.float32) + along) / nbins
    ypos = jnp.broadcast_to(((cell // 16).astype(jnp.float32) + 0.5) / (16.0 * nbins), xpos.shape)
    radius = xpos * xpos + ypos * ypos
    return radius, jnp.ones_like(xpos), -2.0 * xpos, -2.0 * ypos


def place_features(cells):
    cell = np.arange(cells)
    along = (2 * (cell % 16) + 1) / 32.0
    square = along * along
    coarse = np.floor(square * 32) / 32
    up = cell // 16 + 0.5
    return np.stack([np.ones(cells), along, coarse, square - coarse, up, up * up])


def feature_rows(bins, nbins):
    pos = bins.astype(jnp.float32)
    zero, one = jnp.zeros_like(pos), jnp.ones_like(pos)
    inv = one / nbins
    inv2 = inv * inv
    up = inv / 16.0
    unit = [one, zero, zero, zero, zero, zero]
    radius = [pos * pos * inv2, 2.0 * pos * inv2, inv2, inv2, zero, up * up]
    xrow = [pos * inv, inv, zero, zero, zero, zero]
    yrow = [zero, zero, zero, zero, up, zero]
    return jnp.stack([jnp.stack(r, -1) for r in (unit, radius, xrow, yrow)], -1)


def moment_kernel(core, plan, feat_t, feat, out):
    slots, cells = plan.shape[1], plan.shape[2]
    for n in range(plan.shape[0]):
        parts = [
            jnp.dot(feat_t[...], plan[n, k], preferred_element_type=jnp.float32)
            for k in range(slots)
        ]
        out[n] = jnp.dot(
            jnp.concatenate(parts, axis=0), feat[...], preferred_element_type=jnp.float32, precision=HI
        )


def prior_moments(plan, pattern, live, first_bin, total_bins):
    bins, slots, cells = plan.shape[:3]
    half = bins // 2
    core = lax.axis_index("gene")
    rows = 16
    step = math.gcd(half, 3)
    table = np.zeros((rows, cells), np.float32)
    table[:FEATURES] = place_features(cells)
    wide = np.zeros((cells, 128), np.float32)
    wide[:, :rows] = table.T
    raw = pl.pallas_call(
        moment_kernel,
        grid_spec=pltpu.PrefetchScalarGridSpec(
            num_scalar_prefetch=1,
            grid=(half // step,),
            in_specs=[
                pl.BlockSpec(
                    (step, slots, cells, cells), lambda n, c: (c[0] * (half // step) + n, 0, 0, 0)
                ),
                pl.BlockSpec((rows, cells), lambda n, c: (0, 0)),
                pl.BlockSpec((cells, 128), lambda n, c: (0, 0)),
            ],
            out_specs=pl.BlockSpec((step, slots * rows, 128), lambda n, c: (n, 0, 0)),
        ),
        out_shape=jax.ShapeDtypeStruct((half, slots * rows, 128), jnp.float32),
        compiler_params=pltpu.CompilerParams(vmem_limit_bytes=FULL_VMEM),
        cost_estimate=SMALL_COST,
        name="prior_moments",
    )(core[None].astype(jnp.int32), plan, jnp.asarray(table, jnp.bfloat16), jnp.asarray(wide))
    raw = raw.reshape(half, slots, rows, 128)[:, :, :FEATURES, :FEATURES]
    mine = core * half
    own = feature_rows(first_bin + mine + jnp.arange(half, dtype=jnp.int32), total_bins)
    other = feature_rows(lax.dynamic_slice_in_dim(pattern, mine, half), total_bins)
    alive = jnp.arange(slots, dtype=jnp.int32)[None] < lax.dynamic_slice_in_dim(live, mine, half)[:, None]
    right = jnp.sum(raw[..., None] * other[:, :, None, :, :], axis=3)
    right = jnp.sum(jnp.where(alive[:, :, None, None], right, 0.0), axis=1)
    return jnp.sum(own[:, :, :, None] * right[:, :, None, :], axis=(0, 1))


def turn_kernel(source, out):
    genes = source.shape[0]
    out[:, :genes] = source[...].T
    out[:, genes:] = jnp.zeros((out.shape[0], out.shape[1] - genes), out.dtype)


def turned(source, cells):
    genes, width = source.shape
    padded = -(-genes // 128) * 128 + (128 if genes % 128 == 0 else 0)
    step = cells * math.gcd(width // cells, 4)
    return pl.pallas_call(
        turn_kernel,
        grid=(width // step,),
        in_specs=[pl.BlockSpec((genes, step), lambda n: (0, n))],
        out_specs=pl.BlockSpec((step, padded), lambda n: (n, 0)),
        out_shape=jax.ShapeDtypeStruct((width, padded), source.dtype),
        compiler_params=pltpu.CompilerParams(vmem_limit_bytes=FULL_VMEM),
        cost_estimate=SMALL_COST,
        name="turn_source",
    )(source)


def pair_kernel(groups_of, slots, genes, chained, *refs):
    operands = 1 + max(max(own[0], sib[0]) for _, own, sib in groups_of)
    listed, window_of, starts, src_own, src_sib = refs[:5]
    targets = refs[5 : 5 + operands]
    at = 5 + operands
    left, rows = refs[at : at + 2]
    at += 2 + 2 * chained
    e_out, a_out, peak = refs[at : at + 3]
    src_v, tgt_v, a_buf, e_buf, src_sem, tgt_sem, out_sem = refs[at + 3 :]
    cells = a_buf.shape[2]
    last = listed.shape[0] - 1
    total = listed[last]

    fetches = []
    base = 0
    for s, (nbins, *halves) in enumerate(groups_of):
        for side, (operand, half, column) in enumerate(halves):
            columns = pl.ds(column * cells, nbins * cells)
            ref = targets[operand]
            fetches.append(
                pltpu.make_async_copy(
                    ref.at[:, columns] if half is None else ref.at[half, :, columns],
                    tgt_v.at[side, :, base * cells : (base + nbins) * cells],
                    tgt_sem.at[2 * s + side],
                )
            )
        base += nbins
    for fetch in fetches:
        fetch.start()

    def source_copies(n):
        at_n = pl.ds(pl.multiple_of(n * cells, cells), cells)
        return (
            pltpu.make_async_copy(src_own.at[at_n], src_v.at[0, n], src_sem.at[0, n]),
            pltpu.make_async_copy(src_sib.at[at_n], src_v.at[1, n], src_sem.at[1, n]),
        )

    def is_new(p):
        before = listed[jnp.maximum(p - 1, 0)] // slots
        return (p == 0) | (before != listed[p] // slots)

    def begin(p, carry):
        @pl.when(is_new(p))
        def _():
            for copy in source_copies(listed[p] // slots):
                copy.start()

        return carry

    lax.fori_loop(0, total, begin, 0)
    for fetch in fetches:
        fetch.wait()

    def out_copies(half, lane, index):
        return (
            pltpu.make_async_copy(a_buf.at[half, lane], a_out.at[index], out_sem.at[0, half, lane]),
            pltpu.make_async_copy(e_buf.at[half, lane], e_out.at[index], out_sem.at[1, half, lane]),
        )

    def one_pair(index):
        n = index // slots
        w = window_of[index]
        place = jnp.int32(0)
        base = 0
        for s, (nbins, *_) in enumerate(groups_of):
            start = starts[s]
            place = jnp.where((w >= start) & (w < start + nbins), w - start + base, place)
            base += nbins
        columns = pl.ds(pl.multiple_of(place * cells, cells), cells)
        inner = jnp.dot(
            src_v[0, n, :, :genes], tgt_v[0, :, columns], preferred_element_type=jnp.float32
        ) + jnp.dot(
            src_v[1, n, :, :genes], tgt_v[1, :, columns], preferred_element_type=jnp.float32
        )
        lf, rw = left[n], rows[w]
        price = lf[:, 0:1] * rw[0:1]
        for d in range(1, 4):
            price = price + lf[:, d : d + 1] * rw[d : d + 1]
        return inner * (1.0 / (G * EPS)) + price

    def several(group, best):
        half = lax.rem(group, 2)
        first = group * TOGETHER
        for lane in range(TOGETHER):
            p = first + lane

            @pl.when((p < total) & is_new(p))
            def _(p=p):
                for copy in source_copies(listed[p] // slots):
                    copy.wait()

            @pl.when(p - 2 * TOGETHER >= 0)
            def _(lane=lane):
                for copy in out_copies(half, lane, 0):
                    copy.wait()

        picked = [listed[jnp.minimum(first + lane, total - 1)] for lane in range(TOGETHER)]
        exponents = [one_pair(index) for index in picked]
        for lane, (index, arg) in enumerate(zip(picked, exponents)):
            a_buf[half, lane] = arg
            e_buf[half, lane] = jnp.exp(arg)
            best = jnp.maximum(best, jnp.max(jnp.abs(arg).reshape(-1, 8, cells), axis=0))
        for lane, index in enumerate(picked):

            @pl.when(first + lane < total)
            def _(lane=lane, index=index):
                for copy in out_copies(half, lane, index):
                    copy.start()

        return best

    groups = (total + TOGETHER - 1) // TOGETHER
    peak[...] = lax.fori_loop(0, groups, several, jnp.zeros(peak.shape, jnp.float32))
    for back in (2, 1):
        for lane in range(TOGETHER):
            group = groups - back

            @pl.when((group >= 0) & (group * TOGETHER + lane < total))
            def _(lane=lane, group=group):
                for copy in out_copies(lax.rem(group, 2), lane, 0):
                    copy.wait()


def pair_blocks(groups_of, starts, listed, window_of, sources, targets, left, rows, blocks, slots):
    padded = sources[0].shape[1]
    bins, cells = left.shape[:2]
    genes = targets[0].shape[-2]
    width = sum(n for n, *_ in groups_of)
    chained = blocks is not None
    smem = pl.BlockSpec(memory_space=pltpu.SMEM)
    hbm = pl.BlockSpec(memory_space=pltpu.HBM)
    whole = pl.BlockSpec(memory_space=pltpu.VMEM)
    shape = (bins * slots, cells, cells)
    args = [listed, window_of, starts, *sources, *targets, left, rows]
    specs = [smem] * 3 + [hbm] * (2 + len(targets)) + [whole, whole]
    aliases = {}
    if chained:
        aliases = {len(args): 0, len(args) + 1: 1}
        args += [pltpu.with_memory_space_constraint(b, pltpu.HBM) for b in blocks]
        specs += [hbm, hbm]
    e_block, a_block, peak = pl.pallas_call(
        functools.partial(pair_kernel, groups_of, slots, genes, chained),
        in_specs=specs,
        out_specs=[hbm, hbm, whole],
        out_shape=[
            pltpu.HBM(shape, jnp.float32),
            pltpu.HBM(shape, jnp.float32),
            jax.ShapeDtypeStruct((8, cells), jnp.float32),
        ],
        scratch_shapes=[
            pltpu.VMEM((2, bins, cells, padded), jnp.bfloat16),
            pltpu.VMEM((2, genes, width * cells), jnp.bfloat16),
            pltpu.VMEM((2, TOGETHER, cells, cells), jnp.float32),
            pltpu.VMEM((2, TOGETHER, cells, cells), jnp.float32),
            pltpu.SemaphoreType.DMA((2, bins)),
            pltpu.SemaphoreType.DMA((2 * len(groups_of),)),
            pltpu.SemaphoreType.DMA((2, 2, TOGETHER)),
        ],
        input_output_aliases=aliases,
        compiler_params=pltpu.CompilerParams(vmem_limit_bytes=FULL_VMEM),
        cost_estimate=SMALL_COST,
        name="pair_blocks",
    )(*args)
    return (e_block, a_block), peak


def log_sum(terms):
    top = functools.reduce(jnp.maximum, terms)
    return top + jnp.log(sum(jnp.exp(t - top) for t in terms))


def scaling_kernel(bins, slots, first, final, npeaks, *refs):
    tab, live, edges = refs[:3]
    peaks = refs[3 : 3 + npeaks]
    at = 3 + npeaks
    mass, start, log_mass = refs[at : at + 3]
    at += 3
    parts = ()
    if not first:
        parts = refs[at : at + 5]
        at += 5
    e_ref, a_hbm = refs[at : at + 2]
    at += 2
    if first:
        e_hbm, e_ref = e_ref, refs[at]
        at += 1
    if final:
        part_out, low_out, high_out, left_out = refs[at : at + 4]
        at += 4
    else:
        part_out, low_out, high_out, low2_out, high2_out = refs[at : at + 5]
        at += 5
    y_v, v_v, acc_v, x_v, sum_v, load_v, line_v, sem, sems = refs[at:]
    cells = line_v.shape[0]
    steps = 4
    ahead = min(8, bins)

    def bring(n, wait):
        def one(k, inside):
            index = n * slots + k
            copy = pltpu.make_async_copy(e_hbm.at[index], e_ref.at[index], sems.at[n])
            copy.wait() if wait else copy.start()
            return inside

        lax.fori_loop(0, live[n], one, 0)

    if first:
        for n in range(ahead):
            bring(n, False)

    if first:
        v_v[...] = start[...]
    else:
        own, below, above, below2, above2 = parts

        def seen(condition, value):
            return jnp.where(condition, value, MINUS_HUGE)

        low1, high1, low2, high2 = edges[0] > 0, edges[1] > 0, edges[2] > 0, edges[3] > 0
        thirds = (
            (low1, 0, (own[:bins], seen(low1, below[:bins]), seen(low2, below2[...]))),
            (True, bins, (own[bins : 2 * bins], seen(low1, below[bins:]), seen(high1, above[:bins]))),
            (high1, 2 * bins, (own[2 * bins :], seen(high1, above[bins:]), seen(high2, above2[...]))),
        )
        for inside, row, terms in thirds:
            v = log_mass[row : row + bins] - log_sum(terms)
            v_v[row : row + bins] = jnp.where(inside, v, 0.0)
    y_v[...] = jnp.exp(v_v[...])
    acc_v[...] = jnp.zeros_like(acc_v)

    def row_sums(n, carry):
        if first:

            @pl.when(n + ahead < bins)
            def _():
                bring(n + ahead, False)

            bring(n, True)

        def add(step, total):
            for k in range(steps):
                slot = step * steps + k
                index = n * slots + slot
                alive = slot < live[n]
                y = jnp.where(alive, y_v[pl.ds(tab[index], 1)], 0.0)
                total = total + e_ref[jnp.where(alive, index, n * slots)] * y
            return total

        groups = (live[n] + steps - 1) // steps
        sum_v[n] = lax.fori_loop(0, groups, add, jnp.zeros((cells, cells), jnp.float32))
        return carry

    lax.fori_loop(0, bins, row_sums, 0)

    def scale(n, worst):
        total = jnp.sum(sum_v[n], axis=1, keepdims=True)
        x_v[n] = mass[n] / total
        return jnp.maximum(worst, jnp.abs(jnp.log(total)))

    worst = lax.fori_loop(0, bins, scale, jnp.zeros((cells, 1), jnp.float32), unroll=8)

    def column_sums(n, carry):
        x = jnp.broadcast_to(x_v[n], (cells, cells))

        def add(step, inside):
            for k in range(steps):
                slot = step * steps + k
                index = n * slots + slot
                alive = slot < live[n]
                here = jnp.where(alive, index, n * slots)
                part = jnp.sum((e_ref[here] * x).reshape(-1, 8, cells), axis=0)
                acc_v[jnp.where(alive, tab[index], 3 * bins)] += part
            return inside

        lax.fori_loop(0, (live[n] + steps - 1) // steps, add, 0)
        return carry

    lax.fori_loop(0, bins, column_sums, 0)
    column = jnp.sum(acc_v[: 3 * bins], axis=1)
    part_out[...] = jnp.where(
        column > 0, jnp.log(jnp.where(column > 0, column, 1.0)), MINUS_HUGE
    )
    lane = lax.broadcasted_iota(jnp.int32, (cells, cells), 1)
    if final:

        def gather_left(n, table):
            return jnp.where(lane == n, jnp.log(x_v[n]), table)

        table = lax.fori_loop(0, bins, gather_left, jnp.zeros((cells, cells), jnp.float32), unroll=8)
        left_out[...] = table.T[:bins]

    top_peak = functools.reduce(jnp.maximum, [ref[...] for ref in peaks])
    fine = (
        (jnp.max(top_peak) <= PEAK_MAX)
        & (jnp.max(jnp.abs(v_v[...])) <= SCALING_MAX)
        & (jnp.max(worst) <= LOG_SUM_MAX)
    )

    @pl.when(jnp.logical_not(fine))
    def _():
        part_out[...] = jnp.full_like(part_out, MINUS_HUGE)

        def load(index, k):
            copy = pltpu.make_async_copy(a_hbm.at[index], load_v.at[k], sem)
            copy.start()
            copy.wait()

        def one_bin(n, table):
            def bring(k, top):
                index = n * slots + k
                load(index, k)
                return jnp.maximum(top, load_v[k] + v_v[pl.ds(tab[index], 1)])

            top = lax.fori_loop(
                0, live[n], bring, jnp.full((cells, cells), MINUS_HUGE, jnp.float32)
            )
            top = jnp.max(top, axis=1, keepdims=True)

            def add(k, total):
                index = n * slots + k
                return total + jnp.exp(load_v[k] + v_v[pl.ds(tab[index], 1)] - top)

            total = lax.fori_loop(0, live[n], add, jnp.zeros((cells, cells), jnp.float32))
            u = jnp.log(mass[n]) - (top + jnp.log(jnp.sum(total, axis=1, keepdims=True)))

            def columns(k, inside):
                index = n * slots + k
                row = pl.ds(tab[index], 1)
                rating = load_v[k] + u
                best = jnp.max(rating, axis=0, keepdims=True)
                part = best + jnp.log(jnp.sum(jnp.exp(rating - best), axis=0, keepdims=True))
                part_out[row] = log_sum((part_out[row], part))
                return inside

            lax.fori_loop(0, live[n], columns, 0)
            return jnp.where(lane == n, u, table)

        table = lax.fori_loop(0, bins, one_bin, jnp.zeros((cells, cells), jnp.float32))
        if final:
            line_v[...] = table.T
            left_out[...] = line_v[:bins]

    if final:
        low_out[...] = part_out[:bins]
        high_out[...] = part_out[2 * bins :]
    else:
        low_out[...] = part_out[: 2 * bins]
        high_out[...] = part_out[bins:]
        low2_out[...] = part_out[:bins]
        high2_out[...] = part_out[2 * bins :]


def scaling_step(tab, live, edges, peaks, mass, start, log_mass, parts, blocks, slots, final):
    bins = live.shape[0]
    cells = start.shape[1]
    first = not parts
    smem = pl.BlockSpec(memory_space=pltpu.SMEM)
    anywhere = pl.BlockSpec(memory_space=pl.ANY)
    hbm = pl.BlockSpec(memory_space=pltpu.HBM)
    whole = pl.BlockSpec(memory_space=pltpu.VMEM)
    args = [tab, live, edges, *peaks, mass, start, log_mass, *parts]
    args += [
        pltpu.with_memory_space_constraint(blocks[0], pltpu.HBM if first else pltpu.VMEM),
        pltpu.with_memory_space_constraint(blocks[1], pltpu.HBM),
    ]
    specs = [smem] * 3 + [whole] * (len(peaks) + 3 + len(parts)) + [hbm if first else whole, hbm]
    heights = (3, 1, 1, 1) if final else (3, 2, 2, 1, 1)
    return pl.pallas_call(
        functools.partial(scaling_kernel, bins, slots, first, final, len(peaks)),
        in_specs=specs,
        out_specs=[whole] * (first + len(heights)),
        out_shape=[pltpu.VMEM(blocks[0].shape, jnp.float32)] * first
        + [jax.ShapeDtypeStruct((h * bins, cells), jnp.float32) for h in heights],
        scratch_shapes=[
            pltpu.VMEM((3 * bins, cells), jnp.float32),
            pltpu.VMEM((3 * bins, cells), jnp.float32),
            pltpu.VMEM((3 * bins + 1, 8, cells), jnp.float32),
            pltpu.VMEM((bins, cells, 1), jnp.float32),
            pltpu.VMEM((bins, cells, cells), jnp.float32),
            pltpu.VMEM((slots, cells, cells), jnp.float32),
            pltpu.VMEM((cells, cells), jnp.float32),
            pltpu.SemaphoreType.DMA,
            pltpu.SemaphoreType.DMA((bins,)),
        ],
        compiler_params=pltpu.CompilerParams(vmem_limit_bytes=SCALE_VMEM),
        cost_estimate=SMALL_COST,
        name="scaling_step",
    )(*args)


def chunk_bins(bins):
    edges = [round(bins * sum(CHUNKS[:c]) / sum(CHUNKS)) for c in range(len(CHUNKS) + 1)]
    return [(a, b - a) for a, b in zip(edges[:-1], edges[1:]) if b > a]


def shards(source_expr, target_expr, prior_plan, pattern, live, source_mass, target_mass, initial):
    bins, slots, cells = prior_plan.shape[:3]
    tiles = lax.axis_size("tile")
    tile = lax.axis_index("tile")
    total_bins = bins * tiles
    first_bin = tile * bins

    def hop(array, distance):
        pairs = [(i, i + distance) for i in range(tiles) if 0 <= i + distance < tiles]
        return lax.ppermute(array, "tile", pairs)

    def swap(array):
        return lax.ppermute(array, "gene", [(0, 1), (1, 0)])

    chunks = chunk_bins(bins)
    window_of = (pattern - (first_bin - bins)).reshape(-1)
    alive = (jnp.arange(slots, dtype=jnp.int32)[None] < live[:, None]).reshape(-1)
    within = window_of % bins
    step_of = jnp.zeros_like(window_of)
    for c, (start, nbins) in enumerate(chunks):
        step_of = jnp.where((within >= start) & (within < start + nbins), c + 1, step_of)
    step_of = jnp.where(window_of // bins == 1, 0, step_of)
    step_of = jnp.where(alive, step_of, -1)
    pairs = bins * slots
    number = jnp.arange(pairs, dtype=jnp.int32)
    lists = []
    for c in range(len(chunks) + 1):
        chosen = step_of == c
        earlier = number[None, :] < number[:, None]
        rank = jnp.sum((earlier & chosen[None, :]).astype(jnp.int32), axis=1)
        spot = chosen[None, :] & (rank[None, :] == number[:, None])
        listed = jnp.sum(jnp.where(spot, number[None, :], 0), axis=1)
        lists.append(jnp.concatenate([listed, jnp.sum(chosen.astype(jnp.int32))[None]]))

    def after(array, *others):
        return lax.optimization_barrier((array, *others))[0]

    def after2(*arrays):
        return lax.optimization_barrier(arrays)[:2]

    def place(bin_range, *arrays):
        start, nbins = bin_range
        cut = [lax.slice_in_dim(a, start * cells, (start + nbins) * cells, axis=1) for a in arrays]
        return jnp.stack(cut) if len(cut) > 1 else cut[0]

    routes = [(2 * i, 2 * i + 2) for i in range(tiles - 1)]
    routes += [(2 * i + 3, 2 * i + 1) for i in range(tiles - 1)]

    def send(array):
        return lax.ppermute(array, ("tile", "gene"), routes)

    first_own = place(chunks[0], target_expr)
    piece = jnp.stack([first_own, swap(first_own)])
    arrived = [send(piece)]
    prior_plan, target_late = after2(prior_plan, target_expr, piece)
    target_sib = swap(target_late)
    share = prior_moments(prior_plan, pattern, live, first_bin, total_bins)
    copies = jnp.broadcast_to(share, (2 * tiles, *share.shape))
    copies = lax.all_to_all(copies, ("tile", "gene"), split_axis=0, concat_axis=0, tiled=True)
    moments = copies.sum(axis=0)
    scaled = moments / moments[0, 0]
    source_own = turned(after(source_expr, share), cells)
    source_sib = swap(source_own)
    pieces = [None] + [place(c, target_late, target_sib) for c in chunks[1:]]
    arrived.append(send(after(pieces[1], moments)))
    if len(chunks) > 2:
        arrived.append(send(after(pieces[2], arrived[0])))

    own_bins = first_bin + jnp.arange(bins, dtype=jnp.int32)
    window_bins = (first_bin - bins) + jnp.arange(3 * bins, dtype=jnp.int32)
    dist = jnp.stack(place_rows(own_bins, total_bins, cells), axis=-1)
    left = (-THETA / EPS) * jnp.einsum("sid,de->sie", dist, scaled, precision=HI)
    rows = jnp.stack(place_rows(window_bins, total_bins, cells), axis=1)

    sources = (source_own, source_sib)
    blocks, peak = pair_blocks(
        ((bins, (0, None, 0), (1, None, 0)),),
        jnp.full((1,), bins, jnp.int32),
        lists[0],
        window_of,
        sources,
        (target_expr, target_sib),
        left,
        rows,
        None,
        slots,
    )
    peaks = [peak]
    core = lax.axis_index("gene")
    for c, (start, nbins) in enumerate(chunks):
        if c >= 3:
            arrived.append(send(after(pieces[c], arrived[c - 2], peaks[c - 3])))
        mine = arrived[c]
        if c >= 1:
            mine = after(mine, peaks[c - 1])
        groups_of = ((nbins, (0, 0, 0), (0, 1, 0)), (nbins, (1, 1, 0), (1, 0, 0)))
        sides = jnp.stack([start + core * 2 * bins, start + (1 - core) * 2 * bins]).astype(jnp.int32)
        blocks, peak = pair_blocks(
            groups_of,
            sides,
            lists[c + 1],
            window_of,
            sources,
            (mine, swap(mine)),
            left,
            rows,
            blocks,
            slots,
        )
        peaks.append(peak)

    small = after(jnp.stack([initial, jnp.log(target_mass)]), peaks[-3])
    window_small = jnp.concatenate(
        [a.reshape(2, bins, cells) for a in (hop(small, 1), small, hop(small, -1))], axis=1
    )
    start_v, log_mass = window_small[0], window_small[1]
    edges = jnp.stack([tile >= 1, tile < tiles - 1, tile >= 2, tile < tiles - 2]).astype(jnp.int32)
    mass = source_mass.reshape(bins, cells, 1)
    parts = ()
    for step in range(ITERS):
        final = step == ITERS - 1
        out = scaling_step(
            window_of, live, edges, peaks, mass, start_v, log_mass, parts, blocks, slots, final
        )
        if step == 0:
            blocks, out = (out[0], blocks[1]), out[1:]
        own_part, low, high = out[:3]
        below, above = hop(high, 1), hop(low, -1)
        if final:
            left_factors = out[3]
        else:
            parts = (own_part, below, above, hop(out[4], 2), hop(out[3], -2))
    below = jnp.where(edges[0] > 0, below, MINUS_HUGE)
    above = jnp.where(edges[1] > 0, above, MINUS_HUGE)
    right_factors = log_mass[bins : 2 * bins] - log_sum((own_part[bins : 2 * bins], below, above))
    return left_factors.reshape(-1), right_factors.reshape(-1)


def solution(mesh):
    placed = (
        P("gene", "tile"),
        P("gene", "tile"),
        P("tile", None, None, None),
        P("tile", None),
        P("tile"),
        P("tile"),
        P("tile"),
        P("tile"),
    )
    return jax.shard_map(
        shards, mesh=mesh, in_specs=placed, out_specs=(P("tile"), P("tile")), check_vma=False
    )
```

```python
import functools
import math

import jax
import jax.numpy as jnp
import numpy as np
from jax import lax
from jax.experimental import pallas as pl
from jax.experimental.pallas import tpu as pltpu
from jax.sharding import PartitionSpec as P

G = 2000
ITERS = 3
EPS = 0.02
THETA = 0.1
MINUS_HUGE = -1e30
FEATURES = 6
HI = lax.Precision.HIGHEST
FULL_VMEM = 60 * 2**20
SCALE_VMEM = 12 * 2**20
SMALL_COST = pl.CostEstimate(flops=2**20, bytes_accessed=2**16, transcendentals=0)
TOGETHER = 4
CHUNKS = (9, 9, 3, 3)
KERNELS = ((-1, 0), (1,), (2,), (3,))
PEAK_MAX = 30.0
SCALING_MAX = 40.0
LOG_SUM_MAX = 50.0


def place_rows(bins, nbins, cells):
    cell = jnp.arange(cells, dtype=jnp.int32)
    along = ((cell % 16).astype(jnp.float32) + 0.5) / 16.0
    xpos = (bins[..., None].astype(jnp.float32) + along) / nbins
    ypos = jnp.broadcast_to(((cell // 16).astype(jnp.float32) + 0.5) / (16.0 * nbins), xpos.shape)
    radius = xpos * xpos + ypos * ypos
    return radius, jnp.ones_like(xpos), -2.0 * xpos, -2.0 * ypos


def place_features(cells):
    cell = np.arange(cells)
    along = (2 * (cell % 16) + 1) / 32.0
    square = along * along
    coarse = np.floor(square * 32) / 32
    up = cell // 16 + 0.5
    return np.stack([np.ones(cells), along, coarse, square - coarse, up, up * up])


def feature_rows(bins, nbins):
    pos = bins.astype(jnp.float32)
    zero, one = jnp.zeros_like(pos), jnp.ones_like(pos)
    inv = one / nbins
    inv2 = inv * inv
    up = inv / 16.0
    unit = [one, zero, zero, zero, zero, zero]
    radius = [pos * pos * inv2, 2.0 * pos * inv2, inv2, inv2, zero, up * up]
    xrow = [pos * inv, inv, zero, zero, zero, zero]
    yrow = [zero, zero, zero, zero, up, zero]
    return jnp.stack([jnp.stack(r, -1) for r in (unit, radius, xrow, yrow)], -1)


def moment_kernel(core, plan, feat_t, feat, out):
    slots, cells = plan.shape[1], plan.shape[2]
    for n in range(plan.shape[0]):
        parts = [
            jnp.dot(feat_t[...], plan[n, k], preferred_element_type=jnp.float32)
            for k in range(slots)
        ]
        out[n] = jnp.dot(
            jnp.concatenate(parts, axis=0), feat[...], preferred_element_type=jnp.float32, precision=HI
        )


def prior_moments(plan, pattern, live, first_bin, total_bins):
    bins, slots, cells = plan.shape[:3]
    half = bins // 2
    core = lax.axis_index("gene")
    rows = 16
    step = math.gcd(half, 3)
    table = np.zeros((rows, cells), np.float32)
    table[:FEATURES] = place_features(cells)
    wide = np.zeros((cells, 128), np.float32)
    wide[:, :rows] = table.T
    raw = pl.pallas_call(
        moment_kernel,
        grid_spec=pltpu.PrefetchScalarGridSpec(
            num_scalar_prefetch=1,
            grid=(half // step,),
            in_specs=[
                pl.BlockSpec(
                    (step, slots, cells, cells), lambda n, c: (c[0] * (half // step) + n, 0, 0, 0)
                ),
                pl.BlockSpec((rows, cells), lambda n, c: (0, 0)),
                pl.BlockSpec((cells, 128), lambda n, c: (0, 0)),
            ],
            out_specs=pl.BlockSpec((step, slots * rows, 128), lambda n, c: (n, 0, 0)),
        ),
        out_shape=jax.ShapeDtypeStruct((half, slots * rows, 128), jnp.float32),
        compiler_params=pltpu.CompilerParams(vmem_limit_bytes=FULL_VMEM),
        cost_estimate=SMALL_COST,
        name="prior_moments",
    )(core[None].astype(jnp.int32), plan, jnp.asarray(table, jnp.bfloat16), jnp.asarray(wide))
    raw = raw.reshape(half, slots, rows, 128)[:, :, :FEATURES, :FEATURES]
    mine = core * half
    own = feature_rows(first_bin + mine + jnp.arange(half, dtype=jnp.int32), total_bins)
    other = feature_rows(lax.dynamic_slice_in_dim(pattern, mine, half), total_bins)
    alive = jnp.arange(slots, dtype=jnp.int32)[None] < lax.dynamic_slice_in_dim(live, mine, half)[:, None]
    right = jnp.sum(raw[..., None] * other[:, :, None, :, :], axis=3)
    right = jnp.sum(jnp.where(alive[:, :, None, None], right, 0.0), axis=1)
    return jnp.sum(own[:, :, :, None] * right[:, :, None, :], axis=(0, 1))


def turn_kernel(source, out):
    genes = source.shape[0]
    out[:, :genes] = source[...].T
    out[:, genes:] = jnp.zeros((out.shape[0], out.shape[1] - genes), out.dtype)


def turned(source, cells):
    genes, width = source.shape
    padded = -(-genes // 128) * 128 + (128 if genes % 128 == 0 else 0)
    step = cells * math.gcd(width // cells, 4)
    return pl.pallas_call(
        turn_kernel,
        grid=(width // step,),
        in_specs=[pl.BlockSpec((genes, step), lambda n: (0, n))],
        out_specs=pl.BlockSpec((step, padded), lambda n: (n, 0)),
        out_shape=jax.ShapeDtypeStruct((width, padded), source.dtype),
        compiler_params=pltpu.CompilerParams(vmem_limit_bytes=FULL_VMEM),
        cost_estimate=SMALL_COST,
        name="turn_source",
    )(source)


def pair_kernel(groups_of, slots, genes, chained, *refs):
    operands = 1 + max(max(own[0], sib[0]) for _, own, sib in groups_of)
    listed, window_of, starts, src_own, src_sib = refs[:5]
    targets = refs[5 : 5 + operands]
    at = 5 + operands
    left, rows = refs[at : at + 2]
    at += 2 + 2 * chained
    e_out, a_out, peak = refs[at : at + 3]
    src_v, tgt_v, a_buf, e_buf, src_sem, tgt_sem, out_sem = refs[at + 3 :]
    cells = a_buf.shape[2]
    last = listed.shape[0] - 1
    total = listed[last]

    fetches = []
    base = 0
    for s, (nbins, *halves) in enumerate(groups_of):
        for side, (operand, half, column) in enumerate(halves):
            columns = pl.ds(column * cells, nbins * cells)
            ref = targets[operand]
            fetches.append(
                pltpu.make_async_copy(
                    ref.at[:, columns] if half is None else ref.at[half, :, columns],
                    tgt_v.at[side, :, base * cells : (base + nbins) * cells],
                    tgt_sem.at[2 * s + side],
                )
            )
        base += nbins
    for fetch in fetches:
        fetch.start()

    def source_copies(n):
        at_n = pl.ds(pl.multiple_of(n * cells, cells), cells)
        return (
            pltpu.make_async_copy(src_own.at[at_n], src_v.at[0, n], src_sem.at[0, n]),
            pltpu.make_async_copy(src_sib.at[at_n], src_v.at[1, n], src_sem.at[1, n]),
        )

    def is_new(p):
        before = listed[jnp.maximum(p - 1, 0)] // slots
        return (p == 0) | (before != listed[p] // slots)

    def begin(p, carry):
        @pl.when(is_new(p))
        def _():
            for copy in source_copies(listed[p] // slots):
                copy.start()

        return carry

    lax.fori_loop(0, total, begin, 0)
    for fetch in fetches:
        fetch.wait()

    def out_copies(half, lane, index):
        return (
            pltpu.make_async_copy(a_buf.at[half, lane], a_out.at[index], out_sem.at[0, half, lane]),
            pltpu.make_async_copy(e_buf.at[half, lane], e_out.at[index], out_sem.at[1, half, lane]),
        )

    def one_pair(index):
        n = index // slots
        w = window_of[index]
        place = jnp.int32(0)
        base = 0
        for s, (nbins, *_) in enumerate(groups_of):
            start = starts[s]
            place = jnp.where((w >= start) & (w < start + nbins), w - start + base, place)
            base += nbins
        columns = pl.ds(pl.multiple_of(place * cells, cells), cells)
        inner = jnp.dot(
            src_v[0, n, :, :genes], tgt_v[0, :, columns], preferred_element_type=jnp.float32
        ) + jnp.dot(
            src_v[1, n, :, :genes], tgt_v[1, :, columns], preferred_element_type=jnp.float32
        )
        lf, rw = left[n], rows[w]
        price = lf[:, 0:1] * rw[0:1]
        for d in range(1, 4):
            price = price + lf[:, d : d + 1] * rw[d : d + 1]
        return inner * (1.0 / (G * EPS)) + price

    def several(group, best):
        half = lax.rem(group, 2)
        first = group * TOGETHER
        for lane in range(TOGETHER):
            p = first + lane

            @pl.when((p < total) & is_new(p))
            def _(p=p):
                for copy in source_copies(listed[p] // slots):
                    copy.wait()

            @pl.when(p - 2 * TOGETHER >= 0)
            def _(lane=lane):
                for copy in out_copies(half, lane, 0):
                    copy.wait()

        picked = [listed[jnp.minimum(first + lane, total - 1)] for lane in range(TOGETHER)]
        exponents = [one_pair(index) for index in picked]
        for lane, (index, arg) in enumerate(zip(picked, exponents)):
            a_buf[half, lane] = arg
            e_buf[half, lane] = jnp.exp(arg)
            best = jnp.maximum(best, jnp.max(jnp.abs(arg).reshape(-1, 8, cells), axis=0))
        for lane, index in enumerate(picked):

            @pl.when(first + lane < total)
            def _(lane=lane, index=index):
                for copy in out_copies(half, lane, index):
                    copy.start()

        return best

    groups = (total + TOGETHER - 1) // TOGETHER
    peak[...] = lax.fori_loop(0, groups, several, jnp.zeros(peak.shape, jnp.float32))
    for back in (2, 1):
        for lane in range(TOGETHER):
            group = groups - back

            @pl.when((group >= 0) & (group * TOGETHER + lane < total))
            def _(lane=lane, group=group):
                for copy in out_copies(lax.rem(group, 2), lane, 0):
                    copy.wait()


def pair_blocks(groups_of, starts, listed, window_of, sources, targets, left, rows, blocks, slots):
    padded = sources[0].shape[1]
    bins, cells = left.shape[:2]
    genes = targets[0].shape[-2]
    width = sum(n for n, *_ in groups_of)
    chained = blocks is not None
    smem = pl.BlockSpec(memory_space=pltpu.SMEM)
    hbm = pl.BlockSpec(memory_space=pltpu.HBM)
    whole = pl.BlockSpec(memory_space=pltpu.VMEM)
    shape = (bins * slots, cells, cells)
    args = [listed, window_of, starts, *sources, *targets, left, rows]
    specs = [smem] * 3 + [hbm] * (2 + len(targets)) + [whole, whole]
    aliases = {}
    if chained:
        aliases = {len(args): 0, len(args) + 1: 1}
        args += [pltpu.with_memory_space_constraint(b, pltpu.HBM) for b in blocks]
        specs += [hbm, hbm]
    e_block, a_block, peak = pl.pallas_call(
        functools.partial(pair_kernel, groups_of, slots, genes, chained),
        in_specs=specs,
        out_specs=[hbm, hbm, whole],
        out_shape=[
            pltpu.HBM(shape, jnp.float32),
            pltpu.HBM(shape, jnp.float32),
            jax.ShapeDtypeStruct((8, cells), jnp.float32),
        ],
        scratch_shapes=[
            pltpu.VMEM((2, bins, cells, padded), jnp.bfloat16),
            pltpu.VMEM((2, genes, width * cells), jnp.bfloat16),
            pltpu.VMEM((2, TOGETHER, cells, cells), jnp.float32),
            pltpu.VMEM((2, TOGETHER, cells, cells), jnp.float32),
            pltpu.SemaphoreType.DMA((2, bins)),
            pltpu.SemaphoreType.DMA((2 * len(groups_of),)),
            pltpu.SemaphoreType.DMA((2, 2, TOGETHER)),
        ],
        input_output_aliases=aliases,
        compiler_params=pltpu.CompilerParams(vmem_limit_bytes=FULL_VMEM),
        cost_estimate=SMALL_COST,
        name="pair_blocks",
    )(*args)
    return (e_block, a_block), peak


def log_sum(terms):
    top = functools.reduce(jnp.maximum, terms)
    return top + jnp.log(sum(jnp.exp(t - top) for t in terms))


def scaling_kernel(bins, slots, first, final, npeaks, *refs):
    tab, live, edges = refs[:3]
    peaks = refs[3 : 3 + npeaks]
    at = 3 + npeaks
    mass, start, log_mass = refs[at : at + 3]
    at += 3
    parts = ()
    if not first:
        parts = refs[at : at + 3]
        at += 3
    e_ref, a_hbm = refs[at : at + 2]
    at += 2
    if first:
        e_hbm, e_ref = e_ref, refs[at]
        at += 1
    if final:
        part_out, low_out, high_out, left_out = refs[at : at + 4]
        at += 4
    else:
        part_out, near_out, far_out = refs[at : at + 3]
        at += 3
    y_v, v_v, acc_v, x_v, sum_v, load_v, line_v, sem, sems = refs[at:]
    cells = line_v.shape[0]
    steps = 4
    ahead = min(8, bins)

    def bring(n, wait):
        def one(k, inside):
            index = n * slots + k
            copy = pltpu.make_async_copy(e_hbm.at[index], e_ref.at[index], sems.at[n])
            copy.wait() if wait else copy.start()
            return inside

        lax.fori_loop(0, live[n], one, 0)

    if first:
        for n in range(ahead):
            bring(n, False)

    if first:
        v_v[...] = start[...]
    else:
        own, came, passed = parts
        from_below = edges[4] == 0
        nearest = 2 * bins
        below = jnp.where(from_below, came[:nearest], passed[:nearest])
        above = jnp.where(from_below, passed[:nearest], came[:nearest])
        below2 = jnp.where(from_below, came[nearest:], passed[nearest:])
        above2 = jnp.where(from_below, passed[nearest:], came[nearest:])

        def seen(condition, value):
            return jnp.where(condition, value, MINUS_HUGE)

        low1, high1, low2, high2 = edges[0] > 0, edges[1] > 0, edges[2] > 0, edges[3] > 0
        thirds = (
            (low1, 0, (own[:bins], seen(low1, below[:bins]), seen(low2, below2))),
            (True, bins, (own[bins : 2 * bins], seen(low1, below[bins:]), seen(high1, above[:bins]))),
            (high1, 2 * bins, (own[2 * bins :], seen(high1, above[bins:]), seen(high2, above2))),
        )
        for inside, row, terms in thirds:
            v = log_mass[row : row + bins] - log_sum(terms)
            v_v[row : row + bins] = jnp.where(inside, v, 0.0)
    y_v[...] = jnp.exp(v_v[...])
    acc_v[...] = jnp.zeros_like(acc_v)

    def row_sums(n, carry):
        if first:

            @pl.when(n + ahead < bins)
            def _():
                bring(n + ahead, False)

            bring(n, True)

        def add(step, total):
            for k in range(steps):
                slot = step * steps + k
                index = n * slots + slot
                alive = slot < live[n]
                y = jnp.where(alive, y_v[pl.ds(tab[index], 1)], 0.0)
                total = total + e_ref[jnp.where(alive, index, n * slots)] * y
            return total

        groups = (live[n] + steps - 1) // steps
        sum_v[n] = lax.fori_loop(0, groups, add, jnp.zeros((cells, cells), jnp.float32))
        return carry

    lax.fori_loop(0, bins, row_sums, 0)

    def scale(n, worst):
        total = jnp.sum(sum_v[n], axis=1, keepdims=True)
        x_v[n] = mass[n] / total
        return jnp.maximum(worst, jnp.abs(jnp.log(total)))

    worst = lax.fori_loop(0, bins, scale, jnp.zeros((cells, 1), jnp.float32), unroll=8)

    def column_sums(n, carry):
        x = jnp.broadcast_to(x_v[n], (cells, cells))

        def add(step, inside):
            for k in range(steps):
                slot = step * steps + k
                index = n * slots + slot
                alive = slot < live[n]
                here = jnp.where(alive, index, n * slots)
                part = jnp.sum((e_ref[here] * x).reshape(-1, 8, cells), axis=0)
                acc_v[jnp.where(alive, tab[index], 3 * bins)] += part
            return inside

        lax.fori_loop(0, (live[n] + steps - 1) // steps, add, 0)
        return carry

    lax.fori_loop(0, bins, column_sums, 0)
    column = jnp.sum(acc_v[: 3 * bins], axis=1)
    part_out[...] = jnp.where(
        column > 0, jnp.log(jnp.where(column > 0, column, 1.0)), MINUS_HUGE
    )
    lane = lax.broadcasted_iota(jnp.int32, (cells, cells), 1)
    if final:

        def gather_left(n, table):
            return jnp.where(lane == n, jnp.log(x_v[n]), table)

        table = lax.fori_loop(0, bins, gather_left, jnp.zeros((cells, cells), jnp.float32), unroll=8)
        left_out[...] = table.T[:bins]

    top_peak = functools.reduce(jnp.maximum, [ref[...] for ref in peaks])
    fine = (
        (jnp.max(top_peak) <= PEAK_MAX)
        & (jnp.max(jnp.abs(v_v[...])) <= SCALING_MAX)
        & (jnp.max(worst) <= LOG_SUM_MAX)
    )

    @pl.when(jnp.logical_not(fine))
    def _():
        part_out[...] = jnp.full_like(part_out, MINUS_HUGE)

        def load(index, k):
            copy = pltpu.make_async_copy(a_hbm.at[index], load_v.at[k], sem)
            copy.start()
            copy.wait()

        def one_bin(n, table):
            def bring(k, top):
                index = n * slots + k
                load(index, k)
                return jnp.maximum(top, load_v[k] + v_v[pl.ds(tab[index], 1)])

            top = lax.fori_loop(
                0, live[n], bring, jnp.full((cells, cells), MINUS_HUGE, jnp.float32)
            )
            top = jnp.max(top, axis=1, keepdims=True)

            def add(k, total):
                index = n * slots + k
                return total + jnp.exp(load_v[k] + v_v[pl.ds(tab[index], 1)] - top)

            total = lax.fori_loop(0, live[n], add, jnp.zeros((cells, cells), jnp.float32))
            u = jnp.log(mass[n]) - (top + jnp.log(jnp.sum(total, axis=1, keepdims=True)))

            def columns(k, inside):
                index = n * slots + k
                row = pl.ds(tab[index], 1)
                rating = load_v[k] + u
                best = jnp.max(rating, axis=0, keepdims=True)
                part = best + jnp.log(jnp.sum(jnp.exp(rating - best), axis=0, keepdims=True))
                part_out[row] = log_sum((part_out[row], part))
                return inside

            lax.fori_loop(0, live[n], columns, 0)
            return jnp.where(lane == n, u, table)

        table = lax.fori_loop(0, bins, one_bin, jnp.zeros((cells, cells), jnp.float32))
        if final:
            line_v[...] = table.T
            left_out[...] = line_v[:bins]

    if final:
        low_out[...] = part_out[:bins]
        high_out[...] = part_out[2 * bins :]
    else:
        upward = edges[4] == 0
        near_out[...] = jnp.where(upward, part_out[bins:], part_out[: 2 * bins])
        far_out[...] = jnp.where(upward, part_out[2 * bins :], part_out[:bins])


def scaling_step(tab, live, edges, peaks, mass, start, log_mass, parts, blocks, slots, final):
    bins = live.shape[0]
    cells = start.shape[1]
    first = not parts
    smem = pl.BlockSpec(memory_space=pltpu.SMEM)
    anywhere = pl.BlockSpec(memory_space=pl.ANY)
    hbm = pl.BlockSpec(memory_space=pltpu.HBM)
    whole = pl.BlockSpec(memory_space=pltpu.VMEM)
    args = [tab, live, edges, *peaks, mass, start, log_mass, *parts]
    args += [
        pltpu.with_memory_space_constraint(blocks[0], pltpu.HBM if first else pltpu.VMEM),
        pltpu.with_memory_space_constraint(blocks[1], pltpu.HBM),
    ]
    specs = [smem] * 3 + [whole] * (len(peaks) + 3 + len(parts)) + [hbm if first else whole, hbm]
    heights = (3, 1, 1, 1) if final else (3, 2, 1)
    return pl.pallas_call(
        functools.partial(scaling_kernel, bins, slots, first, final, len(peaks)),
        in_specs=specs,
        out_specs=[whole] * (first + len(heights)),
        out_shape=[pltpu.VMEM(blocks[0].shape, jnp.float32)] * first
        + [jax.ShapeDtypeStruct((h * bins, cells), jnp.float32) for h in heights],
        scratch_shapes=[
            pltpu.VMEM((3 * bins, cells), jnp.float32),
            pltpu.VMEM((3 * bins, cells), jnp.float32),
            pltpu.VMEM((3 * bins + 1, 8, cells), jnp.float32),
            pltpu.VMEM((bins, cells, 1), jnp.float32),
            pltpu.VMEM((bins, cells, cells), jnp.float32),
            pltpu.VMEM((slots, cells, cells), jnp.float32),
            pltpu.VMEM((cells, cells), jnp.float32),
            pltpu.SemaphoreType.DMA,
            pltpu.SemaphoreType.DMA((bins,)),
        ],
        compiler_params=pltpu.CompilerParams(vmem_limit_bytes=SCALE_VMEM),
        cost_estimate=SMALL_COST,
        name="scaling_step",
    )(*args)


def chunk_bins(bins):
    edges = [round(bins * sum(CHUNKS[:c]) / sum(CHUNKS)) for c in range(len(CHUNKS) + 1)]
    return [(a, b - a) for a, b in zip(edges[:-1], edges[1:]) if b > a]


def shards(source_expr, target_expr, prior_plan, pattern, live, source_mass, target_mass, initial):
    bins, slots, cells = prior_plan.shape[:3]
    tiles = lax.axis_size("tile")
    tile = lax.axis_index("tile")
    total_bins = bins * tiles
    first_bin = tile * bins

    def hop(array, distance):
        pairs = [(i, i + distance) for i in range(tiles) if 0 <= i + distance < tiles]
        return lax.ppermute(array, "tile", pairs)

    def swap(array):
        return lax.ppermute(array, "gene", [(0, 1), (1, 0)])

    chunks = chunk_bins(bins)
    window_of = (pattern - (first_bin - bins)).reshape(-1)
    alive = (jnp.arange(slots, dtype=jnp.int32)[None] < live[:, None]).reshape(-1)
    within = window_of % bins
    kernel_of = {c: k for k, taken in enumerate(KERNELS) for c in taken}
    step_of = jnp.zeros_like(window_of)
    for c, (start, nbins) in enumerate(chunks):
        step_of = jnp.where((within >= start) & (within < start + nbins), kernel_of[c], step_of)
    step_of = jnp.where(window_of // bins == 1, kernel_of[-1], step_of)
    step_of = jnp.where(alive, step_of, -1)
    pairs = bins * slots
    number = jnp.arange(pairs, dtype=jnp.int32)
    lists = []
    for c in range(len(KERNELS)):
        chosen = step_of == c
        earlier = number[None, :] < number[:, None]
        rank = jnp.sum((earlier & chosen[None, :]).astype(jnp.int32), axis=1)
        spot = chosen[None, :] & (rank[None, :] == number[:, None])
        listed = jnp.sum(jnp.where(spot, number[None, :], 0), axis=1)
        lists.append(jnp.concatenate([listed, jnp.sum(chosen.astype(jnp.int32))[None]]))

    def after(array, *others):
        return lax.optimization_barrier((array, *others))[0]

    def after2(*arrays):
        return lax.optimization_barrier(arrays)[:2]

    def place(bin_range, *arrays):
        start, nbins = bin_range
        cut = [lax.slice_in_dim(a, start * cells, (start + nbins) * cells, axis=1) for a in arrays]
        return jnp.stack(cut) if len(cut) > 1 else cut[0]

    def send(array, far=1):
        routes = [(2 * i, 2 * (i + far)) for i in range(tiles - far)]
        routes += [(2 * (i + far) + 1, 2 * i + 1) for i in range(tiles - far)]
        return lax.ppermute(array, ("tile", "gene"), routes)

    first_own = place(chunks[0], target_expr)
    piece = jnp.stack([first_own, swap(first_own)])
    arrived = [send(piece)]
    prior_plan, target_late = after2(prior_plan, target_expr, piece)
    target_sib = swap(target_late)
    share = prior_moments(prior_plan, pattern, live, first_bin, total_bins)
    copies = jnp.broadcast_to(share, (2 * tiles, *share.shape))
    copies = lax.all_to_all(copies, ("tile", "gene"), split_axis=0, concat_axis=0, tiled=True)
    moments = copies.sum(axis=0)
    scaled = moments / moments[0, 0]
    source_own = turned(after(source_expr, share), cells)
    source_sib = swap(source_own)
    pieces = [None] + [place(c, target_late, target_sib) for c in chunks[1:]]
    small = after(jnp.stack([initial, jnp.log(target_mass)]), share)
    small_low, small_high = hop(small, 1), hop(small, -1)
    window_small = jnp.concatenate(
        [a.reshape(2, bins, cells) for a in (small_low, small, small_high)], axis=1
    )
    start_v, log_mass = window_small[0], window_small[1]
    arrived.append(send(after(pieces[1], moments, small_low, small_high)))
    if len(chunks) > 2:
        arrived.append(send(after(pieces[2], arrived[0])))

    own_bins = first_bin + jnp.arange(bins, dtype=jnp.int32)
    window_bins = (first_bin - bins) + jnp.arange(3 * bins, dtype=jnp.int32)
    dist = jnp.stack(place_rows(own_bins, total_bins, cells), axis=-1)
    left = (-THETA / EPS) * jnp.einsum("sid,de->sie", dist, scaled, precision=HI)
    rows = jnp.stack(place_rows(window_bins, total_bins, cells), axis=1)

    sources = (source_own, source_sib)
    left, *lists = lax.optimization_barrier((left, *lists, *pieces[3:]))[: 1 + len(lists)]
    blocks, peaks = None, []
    core = lax.axis_index("gene")
    for k, taken in enumerate(KERNELS):
        groups_of, starts, targets = [], [], []
        for c in taken:
            at = len(targets)
            if c < 0:
                groups_of.append((bins, (at, None, 0), (at + 1, None, 0)))
                starts.append(jnp.int32(bins))
                targets += [target_expr, target_sib]
                continue
            start, nbins = chunks[c]
            if c >= 3:
                arrived.append(send(after(pieces[c], arrived[c - 2], peaks[0])))
            mine = arrived[c]
            if c in {1: 0, 2: 0, 3: 1}:
                mine = after(mine, peaks[{1: 0, 2: 0, 3: 1}[c]])
            groups_of += [(nbins, (at, 0, 0), (at, 1, 0)), (nbins, (at + 1, 1, 0), (at + 1, 0, 0))]
            starts += [start + core * 2 * bins, start + (1 - core) * 2 * bins]
            targets += [mine, swap(mine)]
        blocks, peak = pair_blocks(
            tuple(groups_of),
            jnp.stack(starts).astype(jnp.int32),
            lists[k],
            window_of,
            sources,
            tuple(targets),
            left,
            rows,
            blocks,
            slots,
        )
        peaks.append(peak)

    edges = [tile >= 1, tile < tiles - 1, tile >= 2, tile < tiles - 2, core == 1]
    edges = jnp.stack(edges).astype(jnp.int32)
    mass = source_mass.reshape(bins, cells, 1)
    parts = ()
    for step in range(ITERS):
        final = step == ITERS - 1
        out = scaling_step(
            window_of, live, edges, peaks, mass, start_v, log_mass, parts, blocks, slots, final
        )
        if step == 0:
            blocks, out = (out[0], blocks[1]), out[1:]
        if not final:
            own_part, near, far = out
            came = jnp.concatenate([send(near), send(far, 2)])
            parts = (own_part, came, swap(came))
    own_part, low, high, left_factors = out
    below, above = hop(high, 1), hop(low, -1)
    below = jnp.where(edges[0] > 0, below, MINUS_HUGE)
    above = jnp.where(edges[1] > 0, above, MINUS_HUGE)
    right_factors = log_mass[bins : 2 * bins] - log_sum((own_part[bins : 2 * bins], below, above))
    return left_factors.reshape(-1), right_factors.reshape(-1)


def solution(mesh):
    placed = (
        P("gene", "tile"),
        P("gene", "tile"),
        P("tile", None, None, None),
        P("tile", None),
        P("tile"),
        P("tile"),
        P("tile"),
        P("tile"),
    )
    return jax.shard_map(
        shards, mesh=mesh, in_specs=placed, out_specs=(P("tile"), P("tile")), check_vma=False
    )
```
